32 devices in a mesh: groups: 2 (over x), tensor: 16 (over z, y, core).
Axes of the slice: x: 2, y: 2, z: 4, core: 2. Of those that a mesh axis runs over, the one named last changes fastest.
Arguments:
- tokens: bfloat16 [256, 4096], P(('groups', 'tensor')), parts along dimension 0, may hold values from -6 to 6
- gate_weight: bfloat16 [14336, 4096], P('tensor'), may hold values from -0.09375 to 0.09375
- up_weight: bfloat16 [14336, 4096], P('tensor'), may hold values from -0.09375 to 0.09375
- down_weight: bfloat16 [14336, 4096], P('tensor'), may hold values from -0.046875 to 0.046875
- cotangent: bfloat16 [256, 4096], P(('groups', 'tensor')), parts along dimension 0, may hold values from -6 to 6
Outputs:
- output: bfloat16 [256, 4096], P(('groups', 'tensor')), parts along dimension 0
- input_grad: bfloat16 [256, 4096], P(('groups', 'tensor')), parts along dimension 0
- gate_grad: bfloat16 [14336, 8192], P('tensor', 'groups'), parts along dimension 1
- up_grad: bfloat16 [14336, 8192], P('tensor', 'groups'), parts along dimension 1
- down_grad: bfloat16 [14336, 8192], P('tensor', 'groups'), parts along dimension 1
The draws below stay inside these ranges and needn't reach their ends.
There are 2 independent parts, one for each index of `groups`. The reference program is written for one: setup_inputs(seed, part) draws one part's arguments, and reference() takes and returns one part's arrays. A program takes and returns all parts, laid end to end along the dimension named above; an argument that names none is the same for every part. Nothing has to cross between parts.
All inputs are finite; a program needn't handle non-finite values.
Results may differ from the reference program's by a relative error of at most 0.0052.
Values may be sent and summed in bfloat16 or wider, within the bound.
No kernel may reach another device: no remote copies, remote signals or barrier semaphores. Data moves between devices by JAX's collectives and lax.ppermute only.
A program may use at most 128 MiB of HBM per device.

```python
import jax
import jax.numpy as jnp

D = 4096
FF = 14336
TOKENS = 128


def level_of(key, shape, pieces, smallest, largest):
    def one(axis_at, parts):
        steps = jax.random.uniform(jax.random.fold_in(jax.random.fold_in(key, 6), axis_at), (parts,), jnp.float32, smallest / len(pieces), largest / len(pieces))
        return jnp.repeat(jnp.exp(steps), shape[axis_at] // parts).reshape((-1,) + (1,) * (len(shape) - axis_at - 1))

    gain = one(*pieces[0])
    for cut in pieces[1:]:
        gain = gain * one(*cut)
    return gain


def normal_values(rng, dims, width, bound, pieces=(), dtype=jnp.bfloat16):
    level = level_of(rng, dims, pieces, -0.22, 0.18) if pieces else 1.0
    entries = jax.random.normal(rng, dims, jnp.float32) * width * level
    return jnp.minimum(jnp.maximum(entries, -bound), bound).astype(dtype)


def setup_inputs(seed: int = 0, part: int = 0) -> dict:
    splits = jax.random.split(jax.random.key(seed), 6)
    part_splits = jax.random.split(jax.random.fold_in(splits[5], part), 6)
    tokens = normal_values(part_splits[0], (TOKENS, D), 1.0, 6.0, ((0, 16),))
    gate_weight = normal_values(splits[1], (FF, D), D ** -0.5, 0.09375, ((0, 16),))
    up_weight = normal_values(splits[2], (FF, D), D ** -0.5, 0.09375, ((0, 16),))
    down_weight = normal_values(splits[3], (FF, D), FF ** -0.5, 0.046875, ((0, 16),))
    cotangent = normal_values(part_splits[4], (TOKENS, D), 1.0, 6.0, ((0, 16),))
    return dict(tokens=tokens, gate_weight=gate_weight, up_weight=up_weight, down_weight=down_weight, cotangent=cotangent)


def rows_by_weight(left, weight):
    return jnp.dot(left, weight.T, preferred_element_type=jnp.float32)


def reference(tokens, gate_weight, up_weight, down_weight, cotangent):
    gate = rows_by_weight(tokens, gate_weight)
    up = rows_by_weight(tokens, up_weight)
    sig = jax.nn.sigmoid(gate)
    act = gate * sig
    hidden = (act * up).astype(jnp.bfloat16)
    output = jnp.dot(hidden, down_weight, preferred_element_type=jnp.float32).astype(jnp.bfloat16)
    d_hidden = rows_by_weight(cotangent, down_weight)
    d_gate = (d_hidden * up * sig * (1.0 + gate * (1.0 - sig))).astype(jnp.bfloat16)
    d_up = (d_hidden * act).astype(jnp.bfloat16)
    summed = jnp.dot(d_gate, gate_weight, preferred_element_type=jnp.float32)
    summed = summed + jnp.dot(d_up, up_weight, preferred_element_type=jnp.float32)
    input_grad = summed.astype(jnp.bfloat16)
    gate_grad = jnp.dot(d_gate.T, tokens, preferred_element_type=jnp.float32).astype(jnp.bfloat16)
    up_grad = jnp.dot(d_up.T, tokens, preferred_element_type=jnp.float32).astype(jnp.bfloat16)
    down_grad = jnp.dot(hidden.T, cotangent, preferred_element_type=jnp.float32).astype(jnp.bfloat16)
    return (output, input_grad, gate_grad, up_grad, down_grad)
```

```python
import jax
import jax.numpy as jnp
from jax import lax
from jax.sharding import PartitionSpec as P

F32 = jnp.float32
BF16 = jnp.bfloat16
CORE = 1


def rows_by_weight(left, weight):
    return lax.dot_general(left, weight, (((1,), (1,)), ((), ())), preferred_element_type=F32)


def over_tokens(left, right):
    return lax.dot_general(left, right, (((0,), (0,)), ((), ())), preferred_element_type=F32)


def stages(n):
    bits = []
    b = n // 2
    while b > 1:
        bits.append(b)
        b //= 2
    return [(e, o) for e, o in zip(bits, bits[-1:] + bits[:-1])] + [(CORE, CORE)]


def swap(x, n, stage):
    return lax.ppermute(x, "tensor", [(i, i ^ stage[i % 2]) for i in range(n)])


def gather(x, n):
    for stage in stages(n):
        x = jnp.concatenate([x, swap(x, n, stage)], 0)
    return x


def scatter_sum(x, n):
    for stage in reversed(stages(n)):
        half = x.shape[0] // 2
        x = x[:half] + swap(x[half:].astype(BF16), n, stage).astype(F32)
    return x.astype(BF16)


def solution(mesh):
    n = mesh.shape["tensor"]

    def per_device(tokens, gate_weight, up_weight, down_weight, cotangent):
        whole = gather(tokens, n)
        grads = gather(cotangent, n)
        gate = rows_by_weight(whole, gate_weight)
        up = rows_by_weight(whole, up_weight)
        sig = jax.nn.sigmoid(gate)
        act = gate * sig
        hidden = (act * up).astype(BF16)
        output = scatter_sum(jnp.dot(hidden, down_weight, preferred_element_type=F32), n)
        d_hidden = rows_by_weight(grads, down_weight)
        d_gate = (d_hidden * up * sig * (1.0 + gate * (1.0 - sig))).astype(BF16)
        d_up = (d_hidden * act).astype(BF16)
        back = jnp.dot(d_gate, gate_weight, preferred_element_type=F32)
        back = back + jnp.dot(d_up, up_weight, preferred_element_type=F32)
        input_grad = scatter_sum(back, n)
        down_grad = over_tokens(hidden, grads).astype(BF16)
        gate_grad = over_tokens(d_gate, whole).astype(BF16)
        up_grad = over_tokens(d_up, whole).astype(BF16)
        return (output, input_grad, gate_grad, up_grad, down_grad)

    rows = P(("groups", "tensor"), None)
    weights = P("tensor", None)
    grads = P("tensor", "groups")
    return jax.shard_map(
        per_device,
        mesh=mesh,
        in_specs=(rows, weights, weights, weights, rows),
        out_specs=(rows, rows, grads, grads, grads),
        check_vma=False,
    )
```

```python
import jax
import jax.numpy as jnp
from jax import lax
from jax.experimental import pallas as pl
from jax.experimental.pallas import tpu as pltpu
from jax.sharding import PartitionSpec as P

F32 = jnp.float32
BF16 = jnp.bfloat16
CORE = 1
CHUNK = 128


def rows_by_weight(left, weight):
    return lax.dot_general(left, weight, (((1,), (1,)), ((), ())), preferred_element_type=F32)


def over_tokens(left, right):
    return lax.dot_general(left, right, (((0,), (0,)), ((), ())), preferred_element_type=F32)


def fetch_kernel(weight, after, held, sem):
    del after
    copy = pltpu.make_async_copy(weight, held, sem)
    copy.start()
    copy.wait()


def fetch(weight, after):
    size = weight.size * weight.dtype.itemsize
    return pl.pallas_call(
        fetch_kernel,
        out_shape=pltpu.VMEM(weight.shape, weight.dtype),
        in_specs=[pl.BlockSpec(memory_space=pl.ANY)] * 2,
        out_specs=pl.BlockSpec(memory_space=pltpu.VMEM),
        scratch_shapes=[pltpu.SemaphoreType.DMA],
        compiler_params=pltpu.CompilerParams(vmem_limit_bytes=16 * 2**20),
        cost_estimate=pl.CostEstimate(flops=0, bytes_accessed=size, transcendentals=0),
    )(weight, after)


def stages(n):
    bits = []
    b = n // 2
    while b > 1:
        bits.append(b)
        b //= 2
    return [(e, o) for e, o in zip(bits, bits[-1:] + bits[:-1])] + [(CORE, CORE)]


def swap(x, n, stage):
    return lax.ppermute(x, "tensor", [(i, i ^ stage[i % 2]) for i in range(n)])


tie = lax.optimization_barrier


def join(own, got):
    return jnp.concatenate([own, got], 0)


def lower(x):
    return x[: x.shape[0] // 2]


def upper(x):
    return x[x.shape[0] // 2 :].astype(BF16)


def add(x, got):
    return lower(x) + got.astype(F32)


def gradient_kernel(left, right, out, held, sems):
    rows = left.shape[1]
    copies = []
    for k, at in enumerate(range(0, rows, CHUNK)):
        part = pl.ds(at, min(CHUNK, rows - at))
        held[part, :] = over_tokens(left[:, part], right[...]).astype(BF16)
        copies.append(pltpu.make_async_copy(held.at[part, :], out.at[part, :], sems.at[k]))
        copies[-1].start()
    for copy in copies:
        copy.wait()


def gradient(left, right):
    rows, width = left.shape[1], right.shape[1]
    return pl.pallas_call(
        gradient_kernel,
        out_shape=jax.ShapeDtypeStruct((rows, width), BF16),
        in_specs=[pl.BlockSpec(memory_space=pltpu.VMEM)] * 2,
        out_specs=pl.BlockSpec(memory_space=pl.ANY),
        scratch_shapes=[pltpu.VMEM((rows, width), BF16), pltpu.SemaphoreType.DMA((pl.cdiv(rows, CHUNK),))],
        compiler_params=pltpu.CompilerParams(vmem_limit_bytes=20 * 2**20),
        cost_estimate=pl.CostEstimate(
            flops=2 * rows * width * left.shape[0], bytes_accessed=2 * rows * width, transcendentals=0
        ),
    )(left, right)


def solution(mesh):
    n = mesh.shape["tensor"]
    there = stages(n)
    back = there[::-1]

    def per_device(tokens, gate_weight, up_weight, down_weight, cotangent):
        t, c = tokens, cotangent
        got, own_t, own_c = tie((swap(t, n, there[0]), fetch(t, t), fetch(c, c)))
        t, c = tie((join(own_t, got), own_c))
        first = True
        for k, (stage, late) in enumerate(zip(there[1:-1], there)):
            got_t, got_c = tie((swap(t, n, stage), swap(cotangent if first else c, n, late)))
            if k == 1:
                got_t, got_c, gate_weight = tie((got_t, got_c, fetch(gate_weight, t)))
            t, c = tie((join(t, got_t), join(c, got_c)))
            first = False
        got_c = swap(c, n, there[-2])
        up_weight = fetch(up_weight, t)
        t = join(t, swap(t, n, there[-1]))
        gate = rows_by_weight(t, gate_weight)
        up = rows_by_weight(t, up_weight)
        sig = jax.nn.sigmoid(gate)
        act = gate * sig
        hidden = (act * up).astype(BF16)
        hidden, got_c = tie((hidden, got_c))
        c = join(c, got_c)
        out, got_c = tie((jnp.dot(hidden, down_weight, preferred_element_type=F32), swap(c, n, there[-1])))
        c = join(c, got_c)

        got = swap(upper(out), n, back[0])
        d_hidden = rows_by_weight(c, down_weight)
        d_gate = (d_hidden * up * sig * (1.0 + gate * (1.0 - sig))).astype(BF16)
        d_up = (d_hidden * act).astype(BF16)
        got, d_gate, d_up = tie((got, d_gate, d_up))
        out = add(out, got)
        out, d_gate, d_up = tie((out, d_gate, d_up))

        got_out = swap(upper(out), n, back[1])
        terms = jnp.dot(d_gate, gate_weight, preferred_element_type=F32)
        terms = terms + jnp.dot(d_up, up_weight, preferred_element_type=F32)
        jobs = [(hidden, c), (d_gate, t), (d_up, t)]
        made = []
        for k, stage in enumerate(back):
            terms, job = tie((terms, jobs[k] if k < 3 else ()))
            got = swap(upper(terms), n, stage)
            work = (gradient(*job),) if job else ()
            got, work, got_out = tie((got, work, got_out))
            made += work
            terms = add(terms, got)
            if k + 1 < len(back):
                out = add(out, got_out)
            got_out = ()
            if k + 2 < len(back):
                terms, out = tie((terms, out))
                got_out = swap(upper(out), n, back[k + 2])
        down_grad, gate_grad, up_grad = made
        return (out.astype(BF16), terms.astype(BF16), gate_grad, up_grad, down_grad)

    rows = P(("groups", "tensor"), None)
    weights = P("tensor", None)
    grads = P("tensor", "groups")
    return jax.shard_map(
        per_device,
        mesh=mesh,
        in_specs=(rows, weights, weights, weights, rows),
        out_specs=(rows, rows, grads, grads, grads),
        check_vma=False,
    )
```

```python
import jax
import jax.numpy as jnp
from jax import lax
from jax.experimental import pallas as pl
from jax.experimental.pallas import tpu as pltpu
from jax.sharding import PartitionSpec as P

F32 = jnp.float32
BF16 = jnp.bfloat16
CORE = 1
CHUNK = 128


def rows_by_weight(left, weight):
    return lax.dot_general(left, weight, (((1,), (1,)), ((), ())), preferred_element_type=F32)


def over_tokens(left, right):
    return lax.dot_general(left, right, (((0,), (0,)), ((), ())), preferred_element_type=F32)


def fetch_kernel(weight, after, held, sem):
    del after
    copy = pltpu.make_async_copy(weight, held, sem)
    copy.start()
    copy.wait()


def fetch(weight, after):
    size = weight.size * weight.dtype.itemsize
    return pl.pallas_call(
        fetch_kernel,
        out_shape=pltpu.VMEM(weight.shape, weight.dtype),
        in_specs=[pl.BlockSpec(memory_space=pl.ANY)] * 2,
        out_specs=pl.BlockSpec(memory_space=pltpu.VMEM),
        scratch_shapes=[pltpu.SemaphoreType.DMA],
        compiler_params=pltpu.CompilerParams(vmem_limit_bytes=16 * 2**20),
        cost_estimate=pl.CostEstimate(flops=0, bytes_accessed=size, transcendentals=0),
    )(weight, after)


def stages(n):
    bits = []
    b = n // 2
    while b > 1:
        bits.append(b)
        b //= 2
    return [(e, o) for e, o in zip(bits, bits[-1:] + bits[:-1])] + [(CORE, CORE)]


def swap(x, n, stage):
    return lax.ppermute(x, "tensor", [(i, i ^ stage[i % 2]) for i in range(n)])


tie = lax.optimization_barrier


def join(own, got):
    return jnp.concatenate([own, got], 0)


def lower(x):
    return x[: x.shape[0] // 2]


def upper(x):
    return x[x.shape[0] // 2 :].astype(BF16)


def add(x, got):
    return lower(x) + got.astype(F32)


def gradient_kernel(left, right, out, held, sems):
    rows = left.shape[1]
    copies = []
    for k, at in enumerate(range(0, rows, CHUNK)):
        part = pl.ds(at, min(CHUNK, rows - at))
        held[part, :] = over_tokens(left[:, part], right[...]).astype(BF16)
        copies.append(pltpu.make_async_copy(held.at[part, :], out.at[part, :], sems.at[k]))
        copies[-1].start()
    for copy in copies:
        copy.wait()


def gradient(left, right):
    rows, width = left.shape[1], right.shape[1]
    return pl.pallas_call(
        gradient_kernel,
        out_shape=jax.ShapeDtypeStruct((rows, width), BF16),
        in_specs=[pl.BlockSpec(memory_space=pltpu.VMEM)] * 2,
        out_specs=pl.BlockSpec(memory_space=pl.ANY),
        scratch_shapes=[pltpu.VMEM((rows, width), BF16), pltpu.SemaphoreType.DMA((pl.cdiv(rows, CHUNK),))],
        compiler_params=pltpu.CompilerParams(vmem_limit_bytes=20 * 2**20),
        cost_estimate=pl.CostEstimate(
            flops=2 * rows * width * left.shape[0], bytes_accessed=2 * rows * width, transcendentals=0
        ),
    )(left, right)


def solution(mesh):
    n = mesh.shape["tensor"]
    there = stages(n)
    back = there[::-1]

    def per_device(tokens, gate_weight, up_weight, down_weight, cotangent):
        t, c = tokens, cotangent
        got, own_t, own_c = tie((swap(t, n, there[0]), fetch(t, t), fetch(c, c)))
        t, c = tie((join(own_t, got), own_c))
        first = True
        for k, (stage, late) in enumerate(zip(there[1:-1], there)):
            got_t, got_c = tie((swap(t, n, stage), swap(cotangent if first else c, n, late)))
            if k == 1:
                got_t, got_c, gate_weight = tie((got_t, got_c, fetch(gate_weight, t)))
            t, c = tie((join(t, got_t), join(c, got_c)))
            first = False
        got_c = swap(c, n, there[-2])
        up_weight = fetch(up_weight, t)
        t = join(t, swap(t, n, there[-1]))
        gate = rows_by_weight(t, gate_weight)
        up = rows_by_weight(t, up_weight)
        sig = jax.nn.sigmoid(gate)
        act = gate * sig
        hidden = (act * up).astype(BF16)
        hidden, got_c = tie((hidden, got_c))
        c = join(c, got_c)
        out, got_c = tie((jnp.dot(hidden, down_weight, preferred_element_type=F32), swap(c, n, there[-1])))
        c = join(c, got_c)

        got = swap(upper(out), n, back[0])
        d_hidden = rows_by_weight(c, down_weight)
        d_gate = (d_hidden * up * sig * (1.0 + gate * (1.0 - sig))).astype(BF16)
        d_up = (d_hidden * act).astype(BF16)
        got, d_gate, d_up = tie((got, d_gate, d_up))
        out = add(out, got)
        out, d_gate, d_up = tie((out, d_gate, d_up))

        terms = jnp.dot(d_gate, gate_weight, preferred_element_type=F32)
        terms = terms + jnp.dot(d_up, up_weight, preferred_element_type=F32)
        terms = add(terms, swap(upper(terms), n, back[0]))
        jobs = [((hidden, c), (d_gate, t)), ((d_up, t),)]
        made = []
        for k in range(1, len(back)):
            terms, job = tie((terms, jobs[k - 1] if k <= 2 else ()))
            sent = jnp.stack([upper(terms), upper(out)])
            got, work = tie((swap(sent, n, back[k]), tuple(gradient(*one) for one in job)))
            made += work
            terms, out = tie((add(terms, got[0]), add(out, got[1])))
        down_grad, gate_grad, up_grad = made
        return (out.astype(BF16), terms.astype(BF16), gate_grad, up_grad, down_grad)

    rows = P(("groups", "tensor"), None)
    weights = P("tensor", None)
    grads = P("tensor", "groups")
    return jax.shard_map(
        per_device,
        mesh=mesh,
        in_specs=(rows, weights, weights, weights, rows),
        out_specs=(rows, rows, grads, grads, grads),
        check_vma=False,
    )
```

```python
import jax
import jax.numpy as jnp
from jax import lax
from jax.experimental import pallas as pl
from jax.experimental.pallas import tpu as pltpu
from jax.sharding import PartitionSpec as P

F32 = jnp.float32
BF16 = jnp.bfloat16
CORE = 1
CHUNK = 128


def rows_by_weight(left, weight):
    return lax.dot_general(left, weight, (((1,), (1,)), ((), ())), preferred_element_type=F32)


def over_tokens(left, right):
    return lax.dot_general(left, right, (((0,), (0,)), ((), ())), preferred_element_type=F32)


def fetch_kernel(weight, after, held, sem):
    del after
    copy = pltpu.make_async_copy(weight, held, sem)
    copy.start()
    copy.wait()


def fetch(weight, after):
    size = weight.size * weight.dtype.itemsize
    return pl.pallas_call(
        fetch_kernel,
        out_shape=pltpu.VMEM(weight.shape, weight.dtype),
        in_specs=[pl.BlockSpec(memory_space=pl.ANY)] * 2,
        out_specs=pl.BlockSpec(memory_space=pltpu.VMEM),
        scratch_shapes=[pltpu.SemaphoreType.DMA],
        compiler_params=pltpu.CompilerParams(vmem_limit_bytes=16 * 2**20),
        cost_estimate=pl.CostEstimate(flops=0, bytes_accessed=size, transcendentals=0),
    )(weight, after)


def stages(n):
    bits = []
    b = n // 2
    while b > 1:
        bits.append(b)
        b //= 2
    return [(e, o) for e, o in zip(bits, bits[-1:] + bits[:-1])] + [(CORE, CORE)]


def swap(x, n, stage):
    return lax.ppermute(x, "tensor", [(i, i ^ stage[i % 2]) for i in range(n)])


tie = lax.optimization_barrier


def join(own, got):
    return jnp.concatenate([own, got], 0)


def lower(x):
    return x[: x.shape[0] // 2]


def upper(x):
    return x[x.shape[0] // 2 :].astype(BF16)


def add(x, got):
    return lower(x) + got.astype(F32)


def gradient_kernel(left, right, out, held, sems):
    rows = left.shape[1]
    copies = []
    for k, at in enumerate(range(0, rows, CHUNK)):
        part = pl.ds(at, min(CHUNK, rows - at))
        held[part, :] = over_tokens(left[:, part], right[...]).astype(BF16)
        copies.append(pltpu.make_async_copy(held.at[part, :], out.at[part, :], sems.at[k]))
        copies[-1].start()
    for copy in copies:
        copy.wait()


def gradient(left, right):
    rows, width = left.shape[1], right.shape[1]
    return pl.pallas_call(
        gradient_kernel,
        out_shape=jax.ShapeDtypeStruct((rows, width), BF16),
        in_specs=[pl.BlockSpec(memory_space=pltpu.VMEM)] * 2,
        out_specs=pl.BlockSpec(memory_space=pl.ANY),
        scratch_shapes=[pltpu.VMEM((rows, width), BF16), pltpu.SemaphoreType.DMA((pl.cdiv(rows, CHUNK),))],
        compiler_params=pltpu.CompilerParams(vmem_limit_bytes=20 * 2**20),
        cost_estimate=pl.CostEstimate(
            flops=2 * rows * width * left.shape[0], bytes_accessed=2 * rows * width, transcendentals=0
        ),
    )(left, right)


def solution(mesh):
    n = mesh.shape["tensor"]
    there = stages(n)
    back = there[::-1]

    def per_device(tokens, gate_weight, up_weight, down_weight, cotangent):
        t, c = tokens, cotangent
        got, own_t, own_c = tie((swap(t, n, there[0]), fetch(t, t), fetch(c, c)))
        t, c = tie((join(own_t, got), own_c))
        for k, (stage, late) in enumerate(zip(there[1:-1], there)):
            got_c = swap(c if k else cotangent, n, late)
            got_t = swap(t, n, stage)
            if k == 1:
                got_t, got_c, gate_weight = tie((got_t, got_c, fetch(gate_weight, t)))
            t = tie(join(t, got_t))
            c = join(c, got_c)
            if k:
                t, c = tie((t, c))
        got_c = swap(c, n, there[-2])
        up_weight = fetch(up_weight, t)
        t = join(t, swap(t, n, there[-1]))
        gate = rows_by_weight(t, gate_weight)
        up = rows_by_weight(t, up_weight)
        sig = jax.nn.sigmoid(gate)
        act = gate * sig
        hidden = (act * up).astype(BF16)
        hidden, got_c = tie((hidden, got_c))
        c = join(c, got_c)
        out, got_c = tie((jnp.dot(hidden, down_weight, preferred_element_type=F32), swap(c, n, there[-1])))
        c = join(c, got_c)

        got = swap(upper(out), n, back[0])
        d_hidden = rows_by_weight(c, down_weight)
        d_gate = (d_hidden * up * sig * (1.0 + gate * (1.0 - sig))).astype(BF16)
        d_up = (d_hidden * act).astype(BF16)
        got, d_gate, d_up = tie((got, d_gate, d_up))
        out = add(out, got)
        out, d_gate, d_up = tie((out, d_gate, d_up))

        terms = jnp.dot(d_gate, gate_weight, preferred_element_type=F32)
        terms = terms + jnp.dot(d_up, up_weight, preferred_element_type=F32)
        terms = add(terms, swap(upper(terms), n, back[0]))
        jobs = [((hidden, c), (d_gate, t)), ((d_up, t),)]
        made = []
        for k in range(1, len(back)):
            terms, job = tie((terms, jobs[k - 1] if k <= 2 else ()))
            sent = jnp.stack([upper(terms), upper(out)])
            got, work = tie((swap(sent, n, back[k]), tuple(gradient(*one) for one in job)))
            made += work
            terms, out = tie((add(terms, got[0]), add(out, got[1])))
        down_grad, gate_grad, up_grad = made
        return (out.astype(BF16), terms.astype(BF16), gate_grad, up_grad, down_grad)

    rows = P(("groups", "tensor"), None)
    weights = P("tensor", None)
    grads = P("tensor", "groups")
    return jax.shard_map(
        per_device,
        mesh=mesh,
        in_specs=(rows, weights, weights, weights, rows),
        out_specs=(rows, rows, grads, grads, grads),
        check_vma=False,
    )
```

```python
import jax
import jax.numpy as jnp
from jax import lax
from jax.experimental import pallas as pl
from jax.experimental.pallas import tpu as pltpu
from jax.sharding import PartitionSpec as P

F32 = jnp.float32
BF16 = jnp.bfloat16
CORE = 1
CHUNK = 128


def rows_by_weight(left, weight):
    return lax.dot_general(left, weight, (((1,), (1,)), ((), ())), preferred_element_type=F32)


def over_tokens(left, right):
    return lax.dot_general(left, right, (((0,), (0,)), ((), ())), preferred_element_type=F32)


def fetch_kernel(weight, after, held, sem):
    del after
    copy = pltpu.make_async_copy(weight, held, sem)
    copy.start()
    copy.wait()


def fetch(weight, after):
    size = weight.size * weight.dtype.itemsize
    return pl.pallas_call(
        fetch_kernel,
        out_shape=pltpu.VMEM(weight.shape, weight.dtype),
        in_specs=[pl.BlockSpec(memory_space=pl.ANY)] * 2,
        out_specs=pl.BlockSpec(memory_space=pltpu.VMEM),
        scratch_shapes=[pltpu.SemaphoreType.DMA],
        compiler_params=pltpu.CompilerParams(vmem_limit_bytes=16 * 2**20),
        cost_estimate=pl.CostEstimate(flops=0, bytes_accessed=size, transcendentals=0),
    )(weight, after)


def stages(n):
    bits = []
    b = n // 2
    while b > 1:
        bits.append(b)
        b //= 2
    return [(e, o) for e, o in zip(bits, bits[-1:] + bits[:-1])] + [(CORE, CORE)]


def swap(x, n, stage):
    return lax.ppermute(x, "tensor", [(i, i ^ stage[i % 2]) for i in range(n)])


tie = lax.optimization_barrier


def join(own, got):
    return jnp.concatenate([own, got], 0)


def lower(x):
    return x[: x.shape[0] // 2]


def upper(x):
    return x[x.shape[0] // 2 :].astype(BF16)


def add(x, got):
    return lower(x) + got.astype(F32)


def gradient_kernel(left, right, out, held, sems):
    rows = left.shape[1]
    copies = []
    for k, at in enumerate(range(0, rows, CHUNK)):
        part = pl.ds(at, min(CHUNK, rows - at))
        held[part, :] = over_tokens(left[:, part], right[...]).astype(BF16)
        copies.append(pltpu.make_async_copy(held.at[part, :], out.at[part, :], sems.at[k]))
        copies[-1].start()
    for copy in copies:
        copy.wait()


def gradient(left, right):
    rows, width = left.shape[1], right.shape[1]
    return pl.pallas_call(
        gradient_kernel,
        out_shape=jax.ShapeDtypeStruct((rows, width), BF16),
        in_specs=[pl.BlockSpec(memory_space=pltpu.VMEM)] * 2,
        out_specs=pl.BlockSpec(memory_space=pl.ANY),
        scratch_shapes=[pltpu.VMEM((rows, width), BF16), pltpu.SemaphoreType.DMA((pl.cdiv(rows, CHUNK),))],
        compiler_params=pltpu.CompilerParams(vmem_limit_bytes=20 * 2**20),
        cost_estimate=pl.CostEstimate(
            flops=2 * rows * width * left.shape[0], bytes_accessed=2 * rows * width, transcendentals=0
        ),
    )(left, right)


def solution(mesh):
    n = mesh.shape["tensor"]
    there = stages(n)
    back = there[::-1]

    def per_device(tokens, gate_weight, up_weight, down_weight, cotangent):
        t, c = tokens, cotangent
        got, own_t, own_c = tie((swap(t, n, there[0]), fetch(t, t), fetch(c, c)))
        t, c = tie((join(own_t, got), own_c))
        for k, (stage, late) in enumerate(zip(there[1:-1], there)):
            got_c = swap(c if k else cotangent, n, late)
            got_t = swap(t, n, stage)
            if k == 1:
                got_t, got_c, up_weight = tie((got_t, got_c, fetch(up_weight, t)))
            t = tie(join(t, got_t))
            c = join(c, got_c)
            if k:
                t, c = tie((t, c))
        got_c = swap(c, n, there[-2])
        t = join(t, swap(t, n, there[-1]))
        gate = rows_by_weight(t, gate_weight)
        up = rows_by_weight(t, up_weight)
        sig = jax.nn.sigmoid(gate)
        act = gate * sig
        hidden = (act * up).astype(BF16)
        hidden, got_c = tie((hidden, got_c))
        c = join(c, got_c)
        out, got_c = tie((jnp.dot(hidden, down_weight, preferred_element_type=F32), swap(c, n, there[-1])))
        c = join(c, got_c)

        got = swap(upper(out), n, back[0])
        d_hidden = rows_by_weight(c, down_weight)
        d_gate = (d_hidden * up * sig * (1.0 + gate * (1.0 - sig))).astype(BF16)
        d_up = (d_hidden * act).astype(BF16)
        got, d_gate, d_up = tie((got, d_gate, d_up))
        out = add(out, got)
        out, d_gate, d_up = tie((out, d_gate, d_up))

        terms = jnp.dot(d_gate, gate_weight, preferred_element_type=F32)
        terms = terms + jnp.dot(d_up, up_weight, preferred_element_type=F32)
        terms = add(terms, swap(upper(terms), n, back[0]))
        jobs = [((hidden, c), (d_gate, t)), ((d_up, t),)]
        made = []
        for k in range(1, len(back)):
            terms, job = tie((terms, jobs[k - 1] if k <= 2 else ()))
            sent = jnp.stack([upper(terms), upper(out)])
            got, work = tie((swap(sent, n, back[k]), tuple(gradient(*one) for one in job)))
            made += work
            terms, out = tie((add(terms, got[0]), add(out, got[1])))
        down_grad, gate_grad, up_grad = made
        return (out.astype(BF16), terms.astype(BF16), gate_grad, up_grad, down_grad)

    rows = P(("groups", "tensor"), None)
    weights = P("tensor", None)
    grads = P("tensor", "groups")
    return jax.shard_map(
        per_device,
        mesh=mesh,
        in_specs=(rows, weights, weights, weights, rows),
        out_specs=(rows, rows, grads, grads, grads),
        check_vma=False,
    )
```

```python
import functools

import jax
import jax.numpy as jnp
from jax import lax
from jax.experimental import pallas as pl
from jax.experimental.pallas import tpu as pltpu
from jax.sharding import PartitionSpec as P

F32 = jnp.float32
BF16 = jnp.bfloat16
CORE = 1
CHUNK = 128


def rows_by_weight(left, weight):
    return lax.dot_general(left, weight, (((1,), (1,)), ((), ())), preferred_element_type=F32)


def over_tokens(left, right):
    return lax.dot_general(left, right, (((0,), (0,)), ((), ())), preferred_element_type=F32)


def fetch_kernel(weight, after, held, sem):
    del after
    copy = pltpu.make_async_copy(weight, held, sem)
    copy.start()
    copy.wait()


def fetch(weight, after):
    size = weight.size * weight.dtype.itemsize
    return pl.pallas_call(
        fetch_kernel,
        out_shape=pltpu.VMEM(weight.shape, weight.dtype),
        in_specs=[pl.BlockSpec(memory_space=pl.ANY)] * 2,
        out_specs=pl.BlockSpec(memory_space=pltpu.VMEM),
        scratch_shapes=[pltpu.SemaphoreType.DMA],
        compiler_params=pltpu.CompilerParams(vmem_limit_bytes=16 * 2**20),
        cost_estimate=pl.CostEstimate(flops=0, bytes_accessed=size, transcendentals=0),
    )(weight, after)


def stages(n):
    bits = []
    b = n // 2
    while b > 1:
        bits.append(b)
        b //= 2
    return [(e, o) for e, o in zip(bits, bits[-1:] + bits[:-1])] + [(CORE, CORE)]


def swap(x, n, stage):
    return lax.ppermute(x, "tensor", [(i, i ^ stage[i % 2]) for i in range(n)])


tie = lax.optimization_barrier


def join(own, got):
    return jnp.concatenate([own, got], 0)


def lower(x):
    return x[: x.shape[0] // 2]


def upper(x):
    return x[x.shape[0] // 2 :].astype(BF16)


def add(x, got):
    return lower(x) + got.astype(F32)


def gradients_kernel(count, *refs):
    pairs, outs, held, sems = refs[: 2 * count], refs[2 * count : 3 * count], refs[-2], refs[-1]
    copies = []
    for job in range(count):
        left, right = pairs[2 * job : 2 * job + 2]
        rows = left.shape[1]
        for k, at in enumerate(range(0, rows, CHUNK)):
            part = pl.ds(at, min(CHUNK, rows - at))
            held[job, part, :] = over_tokens(left[:, part], right[...]).astype(BF16)
            copies.append(pltpu.make_async_copy(held.at[job, part, :], outs[job].at[part, :], sems.at[job, k]))
            copies[-1].start()
    for copy in copies:
        copy.wait()


def gradients(jobs):
    count, rows, width = len(jobs), jobs[0][0].shape[1], jobs[0][1].shape[1]
    return pl.pallas_call(
        functools.partial(gradients_kernel, count),
        out_shape=[jax.ShapeDtypeStruct((rows, width), BF16)] * count,
        in_specs=[pl.BlockSpec(memory_space=pltpu.VMEM)] * (2 * count),
        out_specs=[pl.BlockSpec(memory_space=pl.ANY)] * count,
        scratch_shapes=[
            pltpu.VMEM((count, rows, width), BF16),
            pltpu.SemaphoreType.DMA((count, pl.cdiv(rows, CHUNK))),
        ],
        compiler_params=pltpu.CompilerParams(vmem_limit_bytes=(8 + 10 * count) * 2**20),
        cost_estimate=pl.CostEstimate(
            flops=2 * count * rows * width * jobs[0][0].shape[0], bytes_accessed=2 * count * rows * width, transcendentals=0
        ),
    )(*[ref for job in jobs for ref in job])


def solution(mesh):
    n = mesh.shape["tensor"]
    there = stages(n)
    back = there[::-1]

    def per_device(tokens, gate_weight, up_weight, down_weight, cotangent):
        t, c = tokens, cotangent
        got, own_t, own_c = tie((swap(t, n, there[0]), fetch(t, t), fetch(c, c)))
        t, c = tie((join(own_t, got), own_c))
        for k, (stage, late) in enumerate(zip(there[1:-1], there)):
            got_c = swap(c if k else cotangent, n, late)
            got_t = swap(t, n, stage)
            if k == 1:
                got_t, got_c, up_weight = tie((got_t, got_c, fetch(up_weight, t)))
            t = tie(join(t, got_t))
            c = join(c, got_c)
            if k:
                t, c = tie((t, c))
        got_c = swap(c, n, there[-2])
        t = join(t, swap(t, n, there[-1]))
        gate = rows_by_weight(t, gate_weight)
        up = rows_by_weight(t, up_weight)
        sig = jax.nn.sigmoid(gate)
        act = gate * sig
        hidden = (act * up).astype(BF16)
        hidden, got_c = tie((hidden, got_c))
        c = join(c, got_c)
        out, got_c = tie((jnp.dot(hidden, down_weight, preferred_element_type=F32), swap(c, n, there[-1])))
        c = join(c, got_c)

        got = swap(upper(out), n, back[0])
        d_hidden = rows_by_weight(c, down_weight)
        d_gate = (d_hidden * up * sig * (1.0 + gate * (1.0 - sig))).astype(BF16)
        d_up = (d_hidden * act).astype(BF16)
        got, d_gate, d_up = tie((got, d_gate, d_up))
        out = add(out, got)
        out, d_gate, d_up = tie((out, d_gate, d_up))

        got_out = swap(upper(out), n, back[1])
        terms = jnp.dot(d_gate, gate_weight, preferred_element_type=F32)
        terms = terms + jnp.dot(d_up, up_weight, preferred_element_type=F32)
        terms = add(terms, swap(upper(terms), n, back[0]))
        jobs = [((hidden, c), (d_gate, t)), ((d_up, t),)]
        made = []
        for k in range(1, len(back)):
            terms, job = tie((terms, jobs[k - 1] if k <= 2 else ()))
            sent = upper(terms) if k == 1 else jnp.stack([upper(terms), upper(out)])
            got = swap(sent, n, back[k])
            work = tuple(gradients(job)) if job else ()
            if k == 1:
                got, work, got_out = tie((got, work, got_out))
                out = add(out, got_out)
                terms = add(terms, got)
            else:
                got, work = tie((got, work))
                terms, out = tie((add(terms, got[0]), add(out, got[1])))
            made += work
        down_grad, gate_grad, up_grad = made
        return (out.astype(BF16), terms.astype(BF16), gate_grad, up_grad, down_grad)

    rows = P(("groups", "tensor"), None)
    weights = P("tensor", None)
    grads = P("tensor", "groups")
    return jax.shard_map(
        per_device,
        mesh=mesh,
        in_specs=(rows, weights, weights, weights, rows),
        out_specs=(rows, rows, grads, grads, grads),
        check_vma=False,
    )
```

```python
import functools

import jax
import jax.numpy as jnp
from jax import lax
from jax.experimental import pallas as pl
from jax.experimental.pallas import tpu as pltpu
from jax.sharding import PartitionSpec as P

F32 = jnp.float32
BF16 = jnp.bfloat16
CORE = 1
CHUNK = 128


def rows_by_weight(left, weight):
    return lax.dot_general(left, weight, (((1,), (1,)), ((), ())), preferred_element_type=F32)


def over_tokens(left, right):
    return lax.dot_general(left, right, (((0,), (0,)), ((), ())), preferred_element_type=F32)


def fetch_kernel(weight, after, held, sem):
    del after
    copy = pltpu.make_async_copy(weight, held, sem)
    copy.start()
    copy.wait()


def fetch(weight, after):
    size = weight.size * weight.dtype.itemsize
    return pl.pallas_call(
        fetch_kernel,
        out_shape=pltpu.VMEM(weight.shape, weight.dtype),
        in_specs=[pl.BlockSpec(memory_space=pl.ANY)] * 2,
        out_specs=pl.BlockSpec(memory_space=pltpu.VMEM),
        scratch_shapes=[pltpu.SemaphoreType.DMA],
        compiler_params=pltpu.CompilerParams(vmem_limit_bytes=16 * 2**20),
        cost_estimate=pl.CostEstimate(flops=0, bytes_accessed=size, transcendentals=0),
    )(weight, after)


def stages(n):
    bits = []
    b = n // 2
    while b > 1:
        bits.append(b)
        b //= 2
    return [(e, o) for e, o in zip(bits, bits[-1:] + bits[:-1])] + [(CORE, CORE)]


def swap(x, n, stage):
    return lax.ppermute(x, "tensor", [(i, i ^ stage[i % 2]) for i in range(n)])


tie = lax.optimization_barrier


def join(own, got):
    return jnp.concatenate([own, got], 0)


def lower(x):
    return x[: x.shape[0] // 2]


def upper(x):
    return x[x.shape[0] // 2 :].astype(BF16)


def add(x, got):
    return lower(x) + got.astype(F32)


def gradients_kernel(count, *refs):
    pairs, outs, held, sems = refs[: 2 * count], refs[2 * count : 3 * count], refs[-2], refs[-1]
    copies = []
    for job in range(count):
        left, right = pairs[2 * job : 2 * job + 2]
        rows = left.shape[1]
        for k, at in enumerate(range(0, rows, CHUNK)):
            part = pl.ds(at, min(CHUNK, rows - at))
            held[job, part, :] = over_tokens(left[:, part], right[...]).astype(BF16)
            copies.append(pltpu.make_async_copy(held.at[job, part, :], outs[job].at[part, :], sems.at[job, k]))
            copies[-1].start()
    for copy in copies:
        copy.wait()


def gradients(jobs):
    count, rows, width = len(jobs), jobs[0][0].shape[1], jobs[0][1].shape[1]
    return pl.pallas_call(
        functools.partial(gradients_kernel, count),
        out_shape=[jax.ShapeDtypeStruct((rows, width), BF16)] * count,
        in_specs=[pl.BlockSpec(memory_space=pltpu.VMEM)] * (2 * count),
        out_specs=[pl.BlockSpec(memory_space=pl.ANY)] * count,
        scratch_shapes=[
            pltpu.VMEM((count, rows, width), BF16),
            pltpu.SemaphoreType.DMA((count, pl.cdiv(rows, CHUNK))),
        ],
        compiler_params=pltpu.CompilerParams(vmem_limit_bytes=(8 + 10 * count) * 2**20),
        cost_estimate=pl.CostEstimate(
            flops=2 * count * rows * width * jobs[0][0].shape[0], bytes_accessed=2 * count * rows * width, transcendentals=0
        ),
    )(*[ref for job in jobs for ref in job])


def solution(mesh):
    n = mesh.shape["tensor"]
    there = stages(n)
    back = there[::-1]

    def per_device(tokens, gate_weight, up_weight, down_weight, cotangent):
        t, c = tokens, cotangent
        got, own_t, own_c = tie((swap(t, n, there[0]), fetch(t, t), fetch(c, c)))
        t, c = tie((join(own_t, got), own_c))
        for k, (stage, late) in enumerate(zip(there[1:-1], there)):
            got_c = swap(c if k else cotangent, n, late)
            got_t = swap(t, n, stage)
            if k == 1:
                got_t, got_c, up_weight = tie((got_t, got_c, fetch(up_weight, t)))
            t = tie(join(t, got_t))
            c = join(c, got_c)
            if k:
                t, c = tie((t, c))
        got_c = swap(c, n, there[-2])
        t = join(t, swap(t, n, there[-1]))
        gate = rows_by_weight(t, gate_weight)
        up = rows_by_weight(t, up_weight)
        sig = jax.nn.sigmoid(gate)
        act = gate * sig
        hidden = (act * up).astype(BF16)
        hidden, got_c = tie((hidden, got_c))
        c = join(c, got_c)
        out, got_c = tie((jnp.dot(hidden, down_weight, preferred_element_type=F32), swap(c, n, there[-1])))
        c = join(c, got_c)

        got = swap(upper(out), n, back[0])
        d_hidden = rows_by_weight(c, down_weight)
        d_gate = (d_hidden * up * sig * (1.0 + gate * (1.0 - sig))).astype(BF16)
        d_up = (d_hidden * act).astype(BF16)
        got, d_gate, d_up = tie((got, d_gate, d_up))
        out = add(out, got)
        out, d_gate, d_up = tie((out, d_gate, d_up))

        got_out = swap(upper(out), n, back[1])
        terms = jnp.dot(d_gate, gate_weight, preferred_element_type=F32)
        terms = terms + jnp.dot(d_up, up_weight, preferred_element_type=F32)
        terms = add(terms, swap(upper(terms), n, back[0]))
        jobs = [((hidden, c), (d_gate, t)), ((d_up, t),)]
        made = []
        for k in range(1, len(back)):
            terms, job = tie((terms, jobs[k - 1] if k <= 2 else ()))
            sent = upper(terms) if k == 1 else join(upper(terms), upper(out))
            got = swap(sent, n, back[k])
            work = tuple(gradients(job)) if job else ()
            if k == 1:
                got, work, got_out = tie((got, work, got_out))
                out = add(out, got_out)
                terms = add(terms, got)
            else:
                got, work = tie((got, work))
                terms, out = tie((add(terms, lower(got)), add(out, got[got.shape[0] // 2 :])))
            made += work
        down_grad, gate_grad, up_grad = made
        return (out.astype(BF16), terms.astype(BF16), gate_grad, up_grad, down_grad)

    rows = P(("groups", "tensor"), None)
    weights = P("tensor", None)
    grads = P("tensor", "groups")
    return jax.shard_map(
        per_device,
        mesh=mesh,
        in_specs=(rows, weights, weights, weights, rows),
        out_specs=(rows, rows, grads, grads, grads),
        check_vma=False,
    )
```
